512 devices in a mesh: rep: 32 (over z, x_lo), fsdp: 16 (over y, x_hi, core).
Axes of the slice: x: 4 (x_hi: 2, x_lo: 2; x = x_hi * 2 + x_lo), y: 4, z: 16, core: 2. Of those that a mesh axis runs over, the one named last changes fastest.
Arguments:
- tokens: bfloat16 [32, 2048, 8192], P('rep', 'fsdp'), may hold values from -6 to 6
- key_weight: bfloat16 [32, 1024, 8192], P('rep', None, 'fsdp'), may hold values from -0.0625 to 0.0625
- upstream: bfloat16 [32, 2048, 1024], P('rep', 'fsdp'), may hold values from -6 to 6
- fragment_local: bfloat16 [32, 8, 8, 8192], P('rep', None, None, 'fsdp'), may hold values from -6 to 6
- anchor: float32 [8, 8, 8192], P(None, None, 'fsdp'), may hold values from -6 to 6
- outer_velocity: float32 [8, 8, 8192], P(None, None, 'fsdp'), may hold values from -4 to 4
- fragment_pick: int32 [8], replicated, may hold values from 0 to 7, each once
Outputs:
- keys: bfloat16 [32, 2048, 1024], P('rep', 'fsdp')
- key_grad: bfloat16 [32, 1024, 8192], P('rep', None, 'fsdp')
- new_local: bfloat16 [32, 8, 8, 8192], P('rep', None, None, 'fsdp')
- new_anchor: float32 [8, 8, 8192], P(None, None, 'fsdp')
- new_velocity: float32 [8, 8, 8192], P(None, None, 'fsdp')
The draws below stay inside these ranges and needn't reach their ends.
Inputs may be any that keep to these rules, and one draw needn't show every extreme that they name: `fragment_pick`: a permutation of the 8 fragment indices; its first entry is the fragment whose outer gradient is averaged and applied.
All inputs are finite; a program needn't handle non-finite values.
Results may differ from the reference program's by a relative error of at most 0.019.
Values may be sent and summed in bfloat16 or wider, within the bound.
No kernel may reach another device: no remote copies, remote signals or barrier semaphores. Data moves between devices by JAX's collectives and lax.ppermute only.
A program may use at most 64 MiB of HBM per device.

```python
import jax
import jax.numpy as jnp
from jax import lax

D = 8192
KV = 1024
FRAGS = 8
SLAB_ROWS = 8
TOKENS = 2048
REPLICAS = 32
N_FSDP = 16


def block_levels(rng, shape, pieces, low, top_value):
    def one(dim, blocks):
        draws = jax.random.uniform(jax.random.fold_in(jax.random.fold_in(rng, 6), dim), (blocks,), jnp.float32, low / len(pieces), top_value / len(pieces))
        return jnp.repeat(jnp.exp(draws), shape[dim] // blocks).reshape((-1,) + (1,) * (len(shape) - dim - 1))

    loudness = one(*pieces[0])
    for cut in pieces[1:]:
        loudness = loudness * one(*cut)
    return loudness


def normal_values(stream_key, shape, scale, limit, pieces=(), kind=jnp.bfloat16):
    level = block_levels(stream_key, shape, pieces, -0.22, 0.18) if pieces else 1.0
    entries = jax.random.normal(stream_key, shape, jnp.float32) * scale * level
    return jnp.minimum(jnp.maximum(entries, -limit), limit).astype(kind)


def setup_inputs(seed: int = 0) -> dict:
    splits = jax.random.split(jax.random.key(seed), 8)
    return {
        "tokens": normal_values(splits[0], (REPLICAS, TOKENS, D), 1.0, 6.0, ((0, 32), (1, 16))),
        "key_weight": normal_values(splits[1], (REPLICAS, KV, D), D ** -0.5, 0.0625, ((0, 32), (2, 16))),
        "upstream": normal_values(splits[2], (REPLICAS, TOKENS, KV), 1.0, 6.0, ((0, 32), (1, 16))),
        "fragment_local": normal_values(splits[3], (REPLICAS, FRAGS, SLAB_ROWS, D), 1.0, 6.0, ((0, 32), (3, 16))),
        "anchor": normal_values(splits[4], (FRAGS, SLAB_ROWS, D), 1.0, 6.0, ((2, 16),), jnp.float32),
        "outer_velocity": normal_values(splits[5], (FRAGS, SLAB_ROWS, D), 0.3, 4.0, ((2, 16),), jnp.float32),
        "fragment_pick": jax.random.permutation(splits[6], FRAGS).astype(jnp.int32),
    }


momentum_rate = 0.9
outer_rate = 0.7
merge_weight = 0.5


def inner_step(operands):
    inputs, weight, arriving = operands
    width = inputs.shape[1] // N_FSDP
    keys = jnp.zeros((inputs.shape[0], weight.shape[0]), jnp.float32)
    for block in range(N_FSDP):
        part_in = inputs[:, block * width:(block + 1) * width]
        part_w = weight[:, block * width:(block + 1) * width]
        term = jnp.dot(part_in, part_w.T, preferred_element_type=jnp.float32).astype(jnp.bfloat16)
        term = lax.optimization_barrier(term)
        keys = keys + term.astype(jnp.float32)
    cotangent = (arriving.astype(jnp.float32) * (TOKENS ** -0.5)).astype(jnp.bfloat16)
    grad = jnp.dot(cotangent.T, inputs, preferred_element_type=jnp.float32).astype(jnp.bfloat16)
    return keys.astype(jnp.bfloat16), grad


def reference(tokens, key_weight, upstream, fragment_local, anchor, outer_velocity, fragment_pick):
    keys, key_grad = lax.map(inner_step, (tokens, key_weight, upstream))
    pick = fragment_pick[0]
    anchor_now = lax.dynamic_index_in_dim(anchor, pick, 0, keepdims=False)
    velocity_now = lax.dynamic_index_in_dim(outer_velocity, pick, 0, keepdims=False)
    local_now = lax.dynamic_index_in_dim(fragment_local, pick, 1, keepdims=False)
    delta = jnp.sum(anchor_now[None] - local_now.astype(jnp.float32), axis=0) / REPLICAS
    velocity_new = momentum_rate * velocity_now + delta
    anchor_new = anchor_now - outer_rate * (delta + momentum_rate * velocity_new)
    local_new = (merge_weight * local_now.astype(jnp.float32) + (1.0 - merge_weight) * anchor_new[None]).astype(jnp.bfloat16)
    new_local = lax.dynamic_update_index_in_dim(fragment_local, local_new, pick, 1)
    new_anchor = lax.dynamic_update_index_in_dim(anchor, anchor_new, pick, 0)
    new_velocity = lax.dynamic_update_index_in_dim(outer_velocity, velocity_new, pick, 0)
    return keys, key_grad, new_local, new_anchor, new_velocity
```

```python
import functools

import jax
import jax.numpy as jnp
from jax import lax
from jax.experimental import pallas as pl
from jax.experimental.pallas import tpu as pltpu
from jax.sharding import PartitionSpec as P

momentum_rate = 0.9
outer_rate = 0.7
merge_weight = 0.5

GROUP = 16
SEATS = 4
ROWS = 4
SAME_SEAT = [[row * SEATS + seat for row in range(ROWS)] for seat in range(SEATS)]


def flip(bits):
    return [(i, i ^ bits) for i in range(GROUP)]


def send(value, pairs):
    return lax.ppermute(value, "fsdp", pairs)


def exchange(value):
    return lax.all_to_all(value, "fsdp", 0, 0, axis_index_groups=SAME_SEAT)


def after(value, *others):
    return lax.optimization_barrier((value, *others))[0]


def pack_kernel(scale, cuts, tokens, upstream, *outs):
    width = tokens.shape[1]
    piece = width // GROUP
    seat = lax.rem(lax.axis_index("fsdp"), SEATS)
    cot = (upstream[...].astype(jnp.float32) * scale).astype(jnp.bfloat16)
    for chunk, (low, high) in enumerate(cuts):
        part = high - low
        out = outs[chunk]
        for row in range(ROWS):
            for k in range(SEATS):
                start = pl.multiple_of((row * SEATS + (seat ^ k)) * piece + low, 128)
                out[row, :, k * part : (k + 1) * part] = tokens[:, pl.ds(start, part)]
            if chunk == 0:
                out[row, :, SEATS * part :] = cot


def pack(tokens, upstream, scale, cuts, block=32):
    count, width = tokens.shape
    features = upstream.shape[1]
    cols = [SEATS * (high - low) + (0 if low else features) for low, high in cuts]
    return pl.pallas_call(
        functools.partial(pack_kernel, scale, cuts),
        grid=(count // block,),
        out_shape=[jax.ShapeDtypeStruct((ROWS, count, c), jnp.bfloat16) for c in cols],
        in_specs=[
            pl.BlockSpec((block, width), lambda i: (i, 0)),
            pl.BlockSpec((block, features), lambda i: (i, 0)),
        ],
        out_specs=[pl.BlockSpec((ROWS, block, c), lambda i: (0, i, 0)) for c in cols],
        cost_estimate=pl.CostEstimate(flops=0, bytes_accessed=6 << 20, transcendentals=0),
        name="pack",
    )(tokens, upstream)


def update_kernel(replicas, pick, total, frags, anchor, velocity, new_frags, new_anchor, new_velocity):
    new_frags[...] = frags[...]
    new_anchor[...] = anchor[...]
    new_velocity[...] = velocity[...]
    f = pick[0]
    delta = total[...] / replicas
    velocity_new = momentum_rate * velocity[f] + delta
    anchor_new = anchor[f] - outer_rate * (delta + momentum_rate * velocity_new)
    merged = merge_weight * frags[f].astype(jnp.float32) + (1.0 - merge_weight) * anchor_new
    new_frags[f] = merged.astype(jnp.bfloat16)
    new_anchor[f] = anchor_new
    new_velocity[f] = velocity_new


def update(replicas, pick, total, frags, anchor, velocity):
    return pl.pallas_call(
        functools.partial(update_kernel, replicas),
        out_shape=[jax.ShapeDtypeStruct(a.shape, a.dtype) for a in (frags, anchor, velocity)],
        in_specs=[pl.BlockSpec(memory_space=pltpu.SMEM)] + [pl.BlockSpec(memory_space=pltpu.VMEM)] * 4,
        out_specs=[pl.BlockSpec(memory_space=pltpu.VMEM)] * 3,
        name="update",
    )(pick, total, frags, anchor, velocity)


def local(tokens, key_weight, upstream, fragment_local, anchor, outer_velocity, fragment_pick):
    inputs = tokens[0]
    weight = key_weight[0]
    count, _ = inputs.shape
    features, piece = weight.shape
    scale = (count * lax.axis_size("fsdp")) ** (-0.5)
    (message,) = pack(inputs, upstream[0], scale, ((0, piece),))

    replicas = lax.axis_size("rep")
    pick = fragment_pick[0]
    anchor_now = lax.dynamic_index_in_dim(anchor, pick, 0, keepdims=False)
    local_now = lax.dynamic_index_in_dim(fragment_local[0], pick, 0, keepdims=False)

    def double(total, bit):
        return total + lax.ppermute(total, "rep", [(i, i ^ bit) for i in range(replicas)])

    got = exchange(message)
    weight_x = send(weight, flip(2))
    total = double(after(anchor_now - local_now.astype(jnp.float32), message), 16)
    total = double(total, 8)
    total, weight_x = lax.optimization_barrier((total, weight_x))
    total = double(total, 1)
    weight_c = send(after(weight, message), flip(1))
    weight_xc = send(weight_x, flip(1))
    got = after(got, weight_c, weight_xc, total)

    got = got.reshape(ROWS * count, -1)
    cot = got[:, SEATS * piece :]

    def grad(k):
        return jnp.einsum("tk,tc->kc", cot, got[:, k * piece : (k + 1) * piece], preferred_element_type=jnp.float32)

    far = send(grad(3).astype(jnp.bfloat16), flip(1))
    other = (grad(2) + far.astype(jnp.float32)).astype(jnp.bfloat16)
    other = send(other, flip(2))
    near = send(grad(1).astype(jnp.bfloat16), flip(1))

    weights = jnp.concatenate([weight, weight_c, weight_x, weight_xc], axis=1)
    partial = jnp.einsum("tc,kc->tk", got[:, : SEATS * piece], weights, preferred_element_type=jnp.float32)
    partial = partial.astype(jnp.bfloat16)
    keys = exchange(partial.reshape(ROWS, count, features))
    keys = jnp.sum(keys.astype(jnp.float32), axis=0).astype(jnp.bfloat16)

    total = double(double(after(total, partial), 4), 2)
    new_local, new_anchor, new_velocity = update(
        replicas, fragment_pick, total, fragment_local[0], anchor, outer_velocity
    )
    other = after(other, total, keys)
    own = (grad(0) + near.astype(jnp.float32) + other.astype(jnp.float32)).astype(jnp.bfloat16)
    return (keys[None], own[None], new_local[None], new_anchor, new_velocity)


def solution(mesh):
    return jax.shard_map(
        local,
        mesh=mesh,
        in_specs=(
            P("rep", "fsdp", None),
            P("rep", None, "fsdp"),
            P("rep", "fsdp", None),
            P("rep", None, None, "fsdp"),
            P(None, None, "fsdp"),
            P(None, None, "fsdp"),
            P(),
        ),
        out_specs=(
            P("rep", "fsdp", None),
            P("rep", None, "fsdp"),
            P("rep", None, None, "fsdp"),
            P(None, None, "fsdp"),
            P(None, None, "fsdp"),
        ),
        check_vma=False,
    )
```

```python
import functools

import jax
import jax.numpy as jnp
from jax import lax
from jax.experimental import pallas as pl
from jax.experimental.pallas import tpu as pltpu
from jax.sharding import PartitionSpec as P

momentum_rate = 0.9
outer_rate = 0.7
merge_weight = 0.5

GROUP = 16
SEATS = 4
ROWS = 4
SAME_SEAT = [[row * SEATS + seat for row in range(ROWS)] for seat in range(SEATS)]


def flip(bits):
    return [(i, i ^ bits) for i in range(GROUP)]


def send(value, pairs):
    return lax.ppermute(value, "fsdp", pairs)


def exchange(value):
    return lax.all_to_all(value, "fsdp", 0, 0, axis_index_groups=SAME_SEAT)


def after(value, *others):
    return lax.optimization_barrier((value, *others))[0]


def pack_kernel(scale, cuts, tokens, upstream, *outs):
    width = tokens.shape[1]
    piece = width // GROUP
    seat = lax.rem(lax.axis_index("fsdp"), SEATS)
    cot = (upstream[...].astype(jnp.float32) * scale).astype(jnp.bfloat16)
    for chunk, (low, high) in enumerate(cuts):
        part = high - low
        out = outs[chunk]
        for row in range(ROWS):
            for k in range(SEATS):
                start = pl.multiple_of((row * SEATS + (seat ^ k)) * piece + low, 128)
                out[row, :, k * part : (k + 1) * part] = tokens[:, pl.ds(start, part)]
            if chunk == 0:
                out[row, :, SEATS * part :] = cot


def pack(tokens, upstream, scale, cuts, block=64):
    count, width = tokens.shape
    features = upstream.shape[1]
    cols = [SEATS * (high - low) + (0 if low else features) for low, high in cuts]
    return pl.pallas_call(
        functools.partial(pack_kernel, scale, cuts),
        grid=(count // block,),
        out_shape=[jax.ShapeDtypeStruct((ROWS, count, c), jnp.bfloat16) for c in cols],
        in_specs=[
            pl.BlockSpec((block, width), lambda i: (i, 0)),
            pl.BlockSpec((block, features), lambda i: (i, 0)),
        ],
        out_specs=[pl.BlockSpec((ROWS, block, c), lambda i: (0, i, 0)) for c in cols],
        cost_estimate=pl.CostEstimate(flops=0, bytes_accessed=6 << 20, transcendentals=0),
        name="pack",
    )(tokens, upstream)


def update_kernel(replicas, pick, total, frags, anchor, velocity, new_frags, new_anchor, new_velocity):
    new_frags[...] = frags[...]
    new_anchor[...] = anchor[...]
    new_velocity[...] = velocity[...]
    f = pick[0]
    delta = total[...] / replicas
    velocity_new = momentum_rate * velocity[f] + delta
    anchor_new = anchor[f] - outer_rate * (delta + momentum_rate * velocity_new)
    merged = merge_weight * frags[f].astype(jnp.float32) + (1.0 - merge_weight) * anchor_new
    new_frags[f] = merged.astype(jnp.bfloat16)
    new_anchor[f] = anchor_new
    new_velocity[f] = velocity_new


def update(replicas, pick, total, frags, anchor, velocity):
    return pl.pallas_call(
        functools.partial(update_kernel, replicas),
        out_shape=[jax.ShapeDtypeStruct(a.shape, a.dtype) for a in (frags, anchor, velocity)],
        in_specs=[pl.BlockSpec(memory_space=pltpu.SMEM)] + [pl.BlockSpec(memory_space=pltpu.VMEM)] * 4,
        out_specs=[pl.BlockSpec(memory_space=pltpu.VMEM)] * 3,
        name="update",
    )(pick, total, frags, anchor, velocity)


def local(tokens, key_weight, upstream, fragment_local, anchor, outer_velocity, fragment_pick):
    inputs = tokens[0]
    weight = key_weight[0]
    count, _ = inputs.shape
    features, piece = weight.shape
    scale = (count * lax.axis_size("fsdp")) ** (-0.5)
    (message,) = pack(inputs, upstream[0], scale, ((0, piece),))

    replicas = lax.axis_size("rep")
    pick = fragment_pick[0]
    anchor_now = lax.dynamic_index_in_dim(anchor, pick, 0, keepdims=False)
    local_now = lax.dynamic_index_in_dim(fragment_local[0], pick, 0, keepdims=False)

    def double(total, bit):
        return total + lax.ppermute(total, "rep", [(i, i ^ bit) for i in range(replicas)])

    got = exchange(message)
    weight_x = send(weight, flip(2))
    total = double(after(anchor_now - local_now.astype(jnp.float32), message), 16)
    total = double(total, 8)
    total, weight_x = lax.optimization_barrier((total, weight_x))
    total = double(total, 1)
    weight_c = send(after(weight, message), flip(1))
    weight_xc = send(weight_x, flip(1))
    got = after(got, weight_c, weight_xc, total)

    got = got.reshape(ROWS * count, -1)
    cot = got[:, SEATS * piece :]

    def grad(k):
        return jnp.einsum("tk,tc->kc", cot, got[:, k * piece : (k + 1) * piece], preferred_element_type=jnp.float32)

    far = send(grad(3).astype(jnp.bfloat16), flip(1))
    other = (grad(2) + far.astype(jnp.float32)).astype(jnp.bfloat16)
    other = send(other, flip(2))
    near = send(grad(1).astype(jnp.bfloat16), flip(1))

    weights = jnp.concatenate([weight, weight_c, weight_x, weight_xc], axis=1)
    partial = jnp.einsum("tc,kc->tk", got[:, : SEATS * piece], weights, preferred_element_type=jnp.float32)
    partial = partial.astype(jnp.bfloat16)
    keys = exchange(partial.reshape(ROWS, count, features))
    keys = jnp.sum(keys.astype(jnp.float32), axis=0).astype(jnp.bfloat16)

    total = double(double(after(total, partial), 4), 2)
    new_local, new_anchor, new_velocity = update(
        replicas, fragment_pick, total, fragment_local[0], anchor, outer_velocity
    )
    other = after(other, total, keys)
    own = (grad(0) + near.astype(jnp.float32) + other.astype(jnp.float32)).astype(jnp.bfloat16)
    return (keys[None], own[None], new_local[None], new_anchor, new_velocity)


def solution(mesh):
    return jax.shard_map(
        local,
        mesh=mesh,
        in_specs=(
            P("rep", "fsdp", None),
            P("rep", None, "fsdp"),
            P("rep", "fsdp", None),
            P("rep", None, None, "fsdp"),
            P(None, None, "fsdp"),
            P(None, None, "fsdp"),
            P(),
        ),
        out_specs=(
            P("rep", "fsdp", None),
            P("rep", None, "fsdp"),
            P("rep", None, None, "fsdp"),
            P(None, None, "fsdp"),
            P(None, None, "fsdp"),
        ),
        check_vma=False,
    )
```

```python
import functools

import jax
import jax.numpy as jnp
from jax import lax
from jax.experimental import pallas as pl
from jax.experimental.pallas import tpu as pltpu
from jax.sharding import PartitionSpec as P

momentum_rate = 0.9
outer_rate = 0.7
merge_weight = 0.5

GROUP = 16
SEATS = 4
ROWS = 4
SAME_SEAT = [[row * SEATS + seat for row in range(ROWS)] for seat in range(SEATS)]


def flip(bits):
    return [(i, i ^ bits) for i in range(GROUP)]


def send(value, pairs):
    return lax.ppermute(value, "fsdp", pairs)


def exchange(value):
    return lax.all_to_all(value, "fsdp", 0, 0, axis_index_groups=SAME_SEAT)


def after(value, *others):
    return lax.optimization_barrier((value, *others))[0]


def pack_kernel(scale, cuts, tokens, upstream, *outs):
    width = tokens.shape[1]
    piece = width // GROUP
    seat = lax.rem(lax.axis_index("fsdp"), SEATS)
    cot = (upstream[...].astype(jnp.float32) * scale).astype(jnp.bfloat16)
    for chunk, (low, high) in enumerate(cuts):
        part = high - low
        out = outs[chunk]
        for row in range(ROWS):
            for k in range(SEATS):
                start = pl.multiple_of((row * SEATS + (seat ^ k)) * piece + low, 128)
                out[row, :, k * part : (k + 1) * part] = tokens[:, pl.ds(start, part)]
            if chunk == 0:
                out[row, :, SEATS * part :] = cot


def pack(tokens, upstream, scale, cuts, block=64):
    count, width = tokens.shape
    features = upstream.shape[1]
    cols = [SEATS * (high - low) + (0 if low else features) for low, high in cuts]
    return pl.pallas_call(
        functools.partial(pack_kernel, scale, cuts),
        grid=(count // block,),
        out_shape=[jax.ShapeDtypeStruct((ROWS, count, c), jnp.bfloat16) for c in cols],
        in_specs=[
            pl.BlockSpec((block, width), lambda i: (i, 0)),
            pl.BlockSpec((block, features), lambda i: (i, 0)),
        ],
        out_specs=[pl.BlockSpec((ROWS, block, c), lambda i: (0, i, 0)) for c in cols],
        cost_estimate=pl.CostEstimate(flops=0, bytes_accessed=6 << 20, transcendentals=0),
        name="pack",
    )(tokens, upstream)


def update_kernel(replicas, pick, total, frags, anchor, velocity, new_frags, new_anchor, new_velocity):
    new_frags[...] = frags[...]
    new_anchor[...] = anchor[...]
    new_velocity[...] = velocity[...]
    f = pick[0]
    delta = total[...] / replicas
    velocity_new = momentum_rate * velocity[f] + delta
    anchor_new = anchor[f] - outer_rate * (delta + momentum_rate * velocity_new)
    merged = merge_weight * frags[f].astype(jnp.float32) + (1.0 - merge_weight) * anchor_new
    new_frags[f] = merged.astype(jnp.bfloat16)
    new_anchor[f] = anchor_new
    new_velocity[f] = velocity_new


def update(replicas, pick, total, frags, anchor, velocity):
    return pl.pallas_call(
        functools.partial(update_kernel, replicas),
        out_shape=[jax.ShapeDtypeStruct(a.shape, a.dtype) for a in (frags, anchor, velocity)],
        in_specs=[pl.BlockSpec(memory_space=pltpu.SMEM)] + [pl.BlockSpec(memory_space=pltpu.VMEM)] * 4,
        out_specs=[pl.BlockSpec(memory_space=pltpu.VMEM)] * 3,
        name="update",
    )(pick, total, frags, anchor, velocity)


def finish_kernel(base, other, parts, own, keys, held, result, held_parts, held_keys, sems, out_sems):
    chunks, rows = held.shape[:2]
    blocks, amount, tall = held_parts.shape[:3]
    copies = [(other.at[pl.ds(c * rows, rows)], held.at[c]) for c in range(chunks)]
    copies += [(parts.at[:, pl.ds(n * tall, tall)], held_parts.at[n]) for n in range(blocks)]
    copies = [pltpu.make_async_copy(source, to, sems.at[n]) for n, (source, to) in enumerate(copies)]
    for copy in copies:
        copy.start()
    outs = []

    def leave(source, to):
        outs.append(pltpu.make_async_copy(source, to, out_sems.at[len(outs)]))
        outs[-1].start()

    for c in range(chunks):
        copies[c].wait()
        part = pl.ds(c * rows, rows)
        result[c] = (base[part] + held[c].astype(jnp.float32)).astype(jnp.bfloat16)
        leave(result.at[c], own.at[part])
    for n in range(blocks):
        copies[chunks + n].wait()
        total = held_parts[n, 0].astype(jnp.float32)
        for part in range(1, amount):
            total = total + held_parts[n, part].astype(jnp.float32)
        held_keys[n] = total.astype(jnp.bfloat16)
        leave(held_keys.at[n], keys.at[pl.ds(n * tall, tall)])
    for copy in outs:
        copy.wait()


def finish(base, other, parts, chunks=4, blocks=2):
    rows, cols = base.shape
    amount, count, features = parts.shape
    bf16 = jnp.bfloat16
    return pl.pallas_call(
        finish_kernel,
        out_shape=[jax.ShapeDtypeStruct((rows, cols), bf16), jax.ShapeDtypeStruct((count, features), bf16)],
        in_specs=[pl.BlockSpec(memory_space=pltpu.VMEM)] + [pl.BlockSpec(memory_space=pl.ANY)] * 2,
        out_specs=[pl.BlockSpec(memory_space=pl.ANY)] * 2,
        scratch_shapes=[
            pltpu.VMEM((chunks, rows // chunks, cols), bf16),
            pltpu.VMEM((chunks, rows // chunks, cols), bf16),
            pltpu.VMEM((blocks, amount, count // blocks, features), bf16),
            pltpu.VMEM((blocks, count // blocks, features), bf16),
            pltpu.SemaphoreType.DMA((blocks + chunks,)),
            pltpu.SemaphoreType.DMA((blocks + chunks,)),
        ],
        compiler_params=pltpu.CompilerParams(vmem_limit_bytes=10 << 20),
        cost_estimate=pl.CostEstimate(flops=1 << 20, bytes_accessed=6 << 20, transcendentals=0),
        name="finish",
    )(base, other, parts)


def local(tokens, key_weight, upstream, fragment_local, anchor, outer_velocity, fragment_pick):
    inputs = tokens[0]
    weight = key_weight[0]
    count, _ = inputs.shape
    features, piece = weight.shape
    scale = (count * lax.axis_size("fsdp")) ** (-0.5)
    (message,) = pack(inputs, upstream[0], scale, ((0, piece),))

    replicas = lax.axis_size("rep")
    pick = fragment_pick[0]
    anchor_now = lax.dynamic_index_in_dim(anchor, pick, 0, keepdims=False)
    local_now = lax.dynamic_index_in_dim(fragment_local[0], pick, 0, keepdims=False)

    def double(total, bit):
        return total + lax.ppermute(total, "rep", [(i, i ^ bit) for i in range(replicas)])

    got = exchange(message)
    weight_x = send(weight, flip(2))
    total = double(after(anchor_now - local_now.astype(jnp.float32), message), 16)
    total = double(total, 8)
    total, weight_x = lax.optimization_barrier((total, weight_x))
    total = double(total, 1)
    weight_c = send(after(weight, message), flip(1))
    weight_xc = send(weight_x, flip(1))
    got = after(got, weight_c, weight_xc, total)

    got = got.reshape(ROWS * count, -1)
    cot = got[:, SEATS * piece :]

    def grad(k):
        return jnp.einsum("tk,tc->kc", cot, got[:, k * piece : (k + 1) * piece], preferred_element_type=jnp.float32)

    far = send(grad(3).astype(jnp.bfloat16), flip(1))
    other = (grad(2) + far.astype(jnp.float32)).astype(jnp.bfloat16)
    other = send(other, flip(2))
    near = send(grad(1).astype(jnp.bfloat16), flip(1))

    weights = jnp.concatenate([weight, weight_c, weight_x, weight_xc], axis=1)
    partial = jnp.einsum("tc,kc->tk", got[:, : SEATS * piece], weights, preferred_element_type=jnp.float32)
    partial = partial.astype(jnp.bfloat16)
    keys = exchange(partial.reshape(ROWS, count, features))

    total, near, partial = lax.optimization_barrier((total, near, partial))
    total = double(double(total, 4), 2)
    base = grad(0) + near.astype(jnp.float32)
    new_local, new_anchor, new_velocity = update(
        replicas, fragment_pick, total, fragment_local[0], anchor, outer_velocity
    )
    other, keys, new_anchor = lax.optimization_barrier((other, keys, new_anchor))
    own, keys = finish(base, other, keys)
    return (keys[None], own[None], new_local[None], new_anchor, new_velocity)


def solution(mesh):
    return jax.shard_map(
        local,
        mesh=mesh,
        in_specs=(
            P("rep", "fsdp", None),
            P("rep", None, "fsdp"),
            P("rep", "fsdp", None),
            P("rep", None, None, "fsdp"),
            P(None, None, "fsdp"),
            P(None, None, "fsdp"),
            P(),
        ),
        out_specs=(
            P("rep", "fsdp", None),
            P("rep", None, "fsdp"),
            P("rep", None, None, "fsdp"),
            P(None, None, "fsdp"),
            P(None, None, "fsdp"),
        ),
        check_vma=False,
    )
```

```python
import functools

import jax
import jax.numpy as jnp
from jax import lax
from jax.experimental import pallas as pl
from jax.experimental.pallas import tpu as pltpu
from jax.sharding import PartitionSpec as P

momentum_rate = 0.9
outer_rate = 0.7
merge_weight = 0.5

GROUP = 16
SEATS = 4
ROWS = 4
SAME_SEAT = [[row * SEATS + seat for row in range(ROWS)] for seat in range(SEATS)]


def flip(bits):
    return [(i, i ^ bits) for i in range(GROUP)]


def send(value, pairs):
    return lax.ppermute(value, "fsdp", pairs)


def exchange(value):
    return lax.all_to_all(value, "fsdp", 0, 0, axis_index_groups=SAME_SEAT)


def after(value, *others):
    return lax.optimization_barrier((value, *others))[0]


def pack_kernel(scale, cuts, tokens, upstream, *outs):
    width = tokens.shape[1]
    piece = width // GROUP
    seat = lax.rem(lax.axis_index("fsdp"), SEATS)
    cot = (upstream[...].astype(jnp.float32) * scale).astype(jnp.bfloat16)
    for chunk, (low, high) in enumerate(cuts):
        part = high - low
        out = outs[chunk]
        for row in range(ROWS):
            for k in range(SEATS):
                start = pl.multiple_of((row * SEATS + (seat ^ k)) * piece + low, 128)
                out[row, :, k * part : (k + 1) * part] = tokens[:, pl.ds(start, part)]
            if chunk == 0:
                out[row, :, SEATS * part :] = cot


def pack(tokens, upstream, scale, cuts, block=64):
    count, width = tokens.shape
    features = upstream.shape[1]
    cols = [SEATS * (high - low) + (0 if low else features) for low, high in cuts]
    return pl.pallas_call(
        functools.partial(pack_kernel, scale, cuts),
        grid=(count // block,),
        out_shape=[jax.ShapeDtypeStruct((ROWS, count, c), jnp.bfloat16) for c in cols],
        in_specs=[
            pl.BlockSpec((block, width), lambda i: (i, 0)),
            pl.BlockSpec((block, features), lambda i: (i, 0)),
        ],
        out_specs=[pl.BlockSpec((ROWS, block, c), lambda i: (0, i, 0)) for c in cols],
        cost_estimate=pl.CostEstimate(flops=0, bytes_accessed=6 << 20, transcendentals=0),
        name="pack",
    )(tokens, upstream)


def update_kernel(replicas, pick, total, frags, anchor, velocity, new_frags, new_anchor, new_velocity):
    new_frags[...] = frags[...]
    new_anchor[...] = anchor[...]
    new_velocity[...] = velocity[...]
    f = pick[0]
    delta = total[...] / replicas
    velocity_new = momentum_rate * velocity[f] + delta
    anchor_new = anchor[f] - outer_rate * (delta + momentum_rate * velocity_new)
    merged = merge_weight * frags[f].astype(jnp.float32) + (1.0 - merge_weight) * anchor_new
    new_frags[f] = merged.astype(jnp.bfloat16)
    new_anchor[f] = anchor_new
    new_velocity[f] = velocity_new


def update(replicas, pick, total, frags, anchor, velocity):
    return pl.pallas_call(
        functools.partial(update_kernel, replicas),
        out_shape=[jax.ShapeDtypeStruct(a.shape, a.dtype) for a in (frags, anchor, velocity)],
        in_specs=[pl.BlockSpec(memory_space=pltpu.SMEM)] + [pl.BlockSpec(memory_space=pltpu.VMEM)] * 4,
        out_specs=[pl.BlockSpec(memory_space=pltpu.VMEM)] * 3,
        name="update",
    )(pick, total, frags, anchor, velocity)


def finish_kernel(base, other, parts, own, keys, held_base, held, result, held_parts, held_keys, sems, out_sems):
    chunks, rows = held.shape[:2]
    blocks, amount, tall = held_parts.shape[:3]
    copies = []
    for c in range(chunks):
        part = pl.ds(c * rows, rows)
        copies += [(base.at[part], held_base.at[c]), (other.at[part], held.at[c])]
    copies += [(parts.at[:, pl.ds(n * tall, tall)], held_parts.at[n]) for n in range(blocks)]
    copies = [pltpu.make_async_copy(source, to, sems.at[n]) for n, (source, to) in enumerate(copies)]
    for copy in copies:
        copy.start()
    outs = []

    def leave(source, to):
        outs.append(pltpu.make_async_copy(source, to, out_sems.at[len(outs)]))
        outs[-1].start()

    for c in range(chunks):
        copies[2 * c].wait()
        copies[2 * c + 1].wait()
        part = pl.ds(c * rows, rows)
        result[c] = (held_base[c] + held[c].astype(jnp.float32)).astype(jnp.bfloat16)
        leave(result.at[c], own.at[part])
    for n in range(blocks):
        copies[2 * chunks + n].wait()
        total = held_parts[n, 0].astype(jnp.float32)
        for part in range(1, amount):
            total = total + held_parts[n, part].astype(jnp.float32)
        held_keys[n] = total.astype(jnp.bfloat16)
        leave(held_keys.at[n], keys.at[pl.ds(n * tall, tall)])
    for copy in outs:
        copy.wait()


def finish(base, other, parts, chunks=4, blocks=2):
    rows, cols = base.shape
    amount, count, features = parts.shape
    bf16 = jnp.bfloat16
    return pl.pallas_call(
        finish_kernel,
        out_shape=[jax.ShapeDtypeStruct((rows, cols), bf16), jax.ShapeDtypeStruct((count, features), bf16)],
        in_specs=[pl.BlockSpec(memory_space=pl.ANY)] * 3,
        out_specs=[pl.BlockSpec(memory_space=pl.ANY)] * 2,
        scratch_shapes=[
            pltpu.VMEM((chunks, rows // chunks, cols), jnp.float32),
            pltpu.VMEM((chunks, rows // chunks, cols), bf16),
            pltpu.VMEM((chunks, rows // chunks, cols), bf16),
            pltpu.VMEM((blocks, amount, count // blocks, features), bf16),
            pltpu.VMEM((blocks, count // blocks, features), bf16),
            pltpu.SemaphoreType.DMA((blocks + 2 * chunks,)),
            pltpu.SemaphoreType.DMA((blocks + chunks,)),
        ],
        compiler_params=pltpu.CompilerParams(vmem_limit_bytes=10 << 20),
        cost_estimate=pl.CostEstimate(flops=1 << 20, bytes_accessed=6 << 20, transcendentals=0),
        name="finish",
    )(base, other, parts)


def local(tokens, key_weight, upstream, fragment_local, anchor, outer_velocity, fragment_pick):
    inputs = tokens[0]
    weight = key_weight[0]
    count, _ = inputs.shape
    features, piece = weight.shape
    scale = (count * lax.axis_size("fsdp")) ** (-0.5)
    (message,) = pack(inputs, upstream[0], scale, ((0, piece),))

    replicas = lax.axis_size("rep")
    pick = fragment_pick[0]
    anchor_now = lax.dynamic_index_in_dim(anchor, pick, 0, keepdims=False)
    local_now = lax.dynamic_index_in_dim(fragment_local[0], pick, 0, keepdims=False)

    def double(total, bit):
        return total + lax.ppermute(total, "rep", [(i, i ^ bit) for i in range(replicas)])

    got = exchange(message)
    weight_x = send(weight, flip(2))
    total = double(after(anchor_now - local_now.astype(jnp.float32), message), 16)
    total = double(total, 8)
    total, weight_x = lax.optimization_barrier((total, weight_x))
    total = double(total, 1)
    weight_c = send(after(weight, message), flip(1))
    weight_xc = send(weight_x, flip(1))
    got = after(got, weight_c, weight_xc, total)

    got = got.reshape(ROWS * count, -1)
    cot = got[:, SEATS * piece :]

    def grad(k):
        return jnp.einsum("tk,tc->kc", cot, got[:, k * piece : (k + 1) * piece], preferred_element_type=jnp.float32)

    far = send(grad(3).astype(jnp.bfloat16), flip(1))
    other = (grad(2) + far.astype(jnp.float32)).astype(jnp.bfloat16)
    other = send(other, flip(2))
    near = send(grad(1).astype(jnp.bfloat16), flip(1))

    weights = jnp.concatenate([weight, weight_c, weight_x, weight_xc], axis=1)
    partial = jnp.einsum("tc,kc->tk", got[:, : SEATS * piece], weights, preferred_element_type=jnp.float32)
    partial = partial.astype(jnp.bfloat16)
    keys = exchange(partial.reshape(ROWS, count, features))

    total, near, partial = lax.optimization_barrier((total, near, partial))
    total = double(double(total, 4), 2)
    base = grad(0) + near.astype(jnp.float32)
    new_local, new_anchor, new_velocity = update(
        replicas, fragment_pick, total, fragment_local[0], anchor, outer_velocity
    )
    other, keys, new_anchor = lax.optimization_barrier((other, keys, new_anchor))
    own, keys = finish(base, other, keys)
    return (keys[None], own[None], new_local[None], new_anchor, new_velocity)


def solution(mesh):
    return jax.shard_map(
        local,
        mesh=mesh,
        in_specs=(
            P("rep", "fsdp", None),
            P("rep", None, "fsdp"),
            P("rep", "fsdp", None),
            P("rep", None, None, "fsdp"),
            P(None, None, "fsdp"),
            P(None, None, "fsdp"),
            P(),
        ),
        out_specs=(
            P("rep", "fsdp", None),
            P("rep", None, "fsdp"),
            P("rep", None, None, "fsdp"),
            P(None, None, "fsdp"),
            P(None, None, "fsdp"),
        ),
        check_vma=False,
    )
```
